512 devices in a mesh: row: 16 (over z, core), col: 32 (over y, x).
Axes of the slice: x: 4, y: 8, z: 8, core: 2. Of those that a mesh axis runs over, the one named last changes fastest.
Arguments:
- grad_out: bfloat16 [1536, 16384], P('row', 'col'), may hold values from -1.59375 to 1.59375
- gate_pre: bfloat16 [1536, 13312], P('col', 'row'), may hold values from -10 to 10
- up_pre: bfloat16 [1536, 13312], P('col', 'row'), may hold values from -6 to 6
- down_weight: bfloat16 [13312, 16384], P('row', 'col'), may hold values from -0.046875 to 0.046875
- gate_weight: bfloat16 [16384, 13312], P('col', 'row'), may hold values from -0.09375 to 0.09375
- up_weight: bfloat16 [16384, 13312], P('col', 'row'), may hold values from -0.09375 to 0.09375
Outputs:
- input_grad: bfloat16 [1536, 16384], P('row', 'col')
- down_grad: bfloat16 [13312, 16384], P('row', 'col')
The draws below stay inside these ranges and needn't reach their ends.
All inputs are finite; a program needn't handle non-finite values.
Results may differ from the reference program's by a relative error of at most 0.039.
Values may be sent and summed in bfloat16 or wider, within the bound.
A program may use at most 64 MiB of HBM per device.

```python
import jax
import jax.numpy as jnp
from jax import lax

D = 16384
FF = 13312
TOKENS = 1536
N_ROW = 16
N_COL = 32


def with_spikes(values, key, source, target, blocks, factor):
    owner, partner = [(jnp.arange(values.shape[axis_at]) // (values.shape[axis_at] // blocks)).reshape([-1 if axis == axis_at else 1 for axis in range(values.ndim)]) for axis_at in (source, target)]
    chosen = jax.random.permutation(key, blocks)[partner]
    strong = (owner == chosen) | (owner == (partner + blocks // 2) % blocks)
    return jnp.where(strong, factor * values, values)


def steps_of(own_key, shape, split, low, largest):
    level = 1.0
    for dim, blocks in split:
        draws = jax.random.uniform(jax.random.fold_in(jax.random.fold_in(own_key, 6), dim), (blocks,), jnp.float32, low / len(split), largest / len(split))
        level = level * jnp.repeat(jnp.exp(draws), shape[dim] // blocks).reshape((-1,) + (1,) * (len(shape) - 1 - dim))
    return level


def centred(rng, shape, spread, most, split=(), held_as=jnp.bfloat16):
    result = jax.random.normal(rng, shape, jnp.float32) * spread
    if len(split) > 0:
        result = steps_of(rng, shape, split, -0.22, 0.18) * result
    return jnp.clip(result, min=-most, max=most).astype(held_as)


def bell_draw_with(own_key, extent, deviation, bound, shards, heavy, held_as=jnp.bfloat16):
    result = deviation * jax.random.normal(own_key, extent, jnp.float32)
    if shards:
        result = result * steps_of(own_key, extent, shards, -0.22, 0.18)
    return jnp.clip(with_spikes(result, jax.random.fold_in(own_key, 3), *heavy), -bound, bound).astype(held_as)


def setup_inputs(seed: int = 0) -> dict:
    arg_keys = jax.random.split(jax.random.key(seed), 7)
    grad_out = bell_draw_with(arg_keys[0], (TOKENS, D), 0.2, 1.59375, ((0, 16), (1, 32)), (1, 0, 32, 2.75))
    gate_pre = centred(arg_keys[1], (TOKENS, FF), 2.0, 10.0, ((0, 32), (1, 16)))
    up_pre = centred(arg_keys[2], (TOKENS, FF), 1.0, 6.0, ((0, 32), (1, 16)))
    down_weight = centred(arg_keys[3], (FF, D), D ** -0.5, 0.046875, ((0, 16), (1, 32)))
    gate_weight = bell_draw_with(arg_keys[4], (D, FF), FF ** -0.5, 0.09375, ((0, 32), (1, 16)), (1, 0, 32, 2.75))
    up_weight = bell_draw_with(arg_keys[5], (D, FF), FF ** -0.5, 0.09375, ((0, 32), (1, 16)), (1, 0, 32, 2.75))
    return {"grad_out": grad_out, "gate_pre": gate_pre, "up_pre": up_pre, "down_weight": down_weight, "gate_weight": gate_weight, "up_weight": up_weight}


def reference(grad_out, gate_pre, up_pre, down_weight, gate_weight, up_weight):
    block_width = D // N_COL

    def add_block(summed, block_index):
        offset = (block_index * block_width).astype(jnp.int32)
        grad_block = lax.dynamic_slice_in_dim(grad_out, offset, block_width, 1)
        weight_block = lax.dynamic_slice_in_dim(down_weight, offset, block_width, 1)
        partial_value = lax.dot_general(grad_block, weight_block, (((1,), (1,)), ((), ())), preferred_element_type=jnp.float32)
        partial_value = lax.optimization_barrier(partial_value.astype(jnp.bfloat16)).astype(jnp.float32)
        return summed + partial_value, None

    hidden_grad, _ = lax.scan(add_block, jnp.zeros((TOKENS, FF), jnp.float32), jnp.arange(N_COL, dtype=jnp.int32))
    gate_value = gate_pre.astype(jnp.float32)
    up_value = up_pre.astype(jnp.float32)
    sigmoid_gate = jax.nn.sigmoid(gate_value)
    activated = gate_value * sigmoid_gate
    hidden = (activated * up_value).astype(jnp.bfloat16)
    up_grad = (hidden_grad * activated).astype(jnp.bfloat16)
    gate_grad = (hidden_grad * up_value * sigmoid_gate * (1.0 + gate_value * (1.0 - sigmoid_gate))).astype(jnp.bfloat16)
    down_grad = lax.dot_general(hidden, grad_out, (((0,), (0,)), ((), ())), preferred_element_type=jnp.float32).astype(jnp.bfloat16)
    unit_width = FF // N_ROW

    def add_units(summed, block_index):
        offset = (block_index * unit_width).astype(jnp.int32)
        gate_block = lax.dynamic_slice_in_dim(gate_grad, offset, unit_width, 1)
        up_block = lax.dynamic_slice_in_dim(up_grad, offset, unit_width, 1)
        gate_rows = lax.dynamic_slice_in_dim(gate_weight, offset, unit_width, 1)
        up_rows = lax.dynamic_slice_in_dim(up_weight, offset, unit_width, 1)
        partial_value = lax.dot_general(gate_block, gate_rows, (((1,), (1,)), ((), ())), preferred_element_type=jnp.float32)
        partial_value = partial_value + lax.dot_general(up_block, up_rows, (((1,), (1,)), ((), ())), preferred_element_type=jnp.float32)
        partial_value = lax.optimization_barrier(partial_value.astype(jnp.bfloat16)).astype(jnp.float32)
        return summed + partial_value, None

    input_grad, _ = lax.scan(add_units, jnp.zeros((TOKENS, D), jnp.float32), jnp.arange(N_ROW, dtype=jnp.int32))
    return input_grad.astype(jnp.bfloat16), down_grad
```

```python
import functools

import jax
import jax.numpy as jnp
from jax import lax
from jax.experimental import pallas as pl
from jax.experimental.pallas import tpu as pltpu
from jax.sharding import PartitionSpec as P

NZ, NY, NX = 8, 8, 4
TOK = 48
PAIR = 96
UNITS = 832
WIDE = 2 * UNITS
HEAD = 768
FEAT = 512
MESH = pl.DeviceIdType.MESH
F32, BF16 = jnp.float32, jnp.bfloat16


def wrap(value, size):
    return lax.rem(value + 2 * size, size)


class Tree:
    def __init__(self, first, z2, y, x):
        self.first = first
        self.row = z2
        self.na, self.nb = (NY, NX) if first == "y" else (NX, NY)
        self.a, self.b = (y, x) if first == "y" else (x, y)
        self.la, self.lb = self.na // 2, self.nb // 2

    def offsets(self, dist):
        if dist == 0:
            return [0]
        if dist == self.la:
            return [dist]
        return [dist, -dist]

    def sign_b(self, d, side):
        sign = 1 if d % 2 == 0 else -1
        return sign if side == 0 else -sign

    def len_a(self, side):
        return self.la - side

    def len_b(self, side):
        return self.lb - side

    def at_a(self, off):
        return wrap(self.a + off, self.na)

    def at_b(self, off):
        return wrap(self.b + off, self.nb)

    def yx(self, off_a, off_b):
        ia, ib = self.at_a(off_a), self.at_b(off_b)
        return (ia, ib) if self.first == "y" else (ib, ia)

    def device(self, off_a, off_b):
        iy, ix = self.yx(off_a, off_b)
        return (self.row, iy * NX + ix)


def side_of(d):
    return 0 if d > 0 else 1


class Gather:
    def __init__(self, tree, buf, s1, r1, s2, r2):
        self.t, self.buf = tree, buf
        self.s1, self.r1, self.s2, self.r2 = s1, r1, s2, r2

    def copy_a(self, side, hop):
        t = self.t
        sgn = 1 - 2 * side
        iy, ix = t.yx(-sgn * (hop - 1), 0)
        ref = self.buf.at[iy, ix]
        return pltpu.make_async_remote_copy(
            src_ref=ref, dst_ref=ref, send_sem=self.s1.at[side, hop - 1], recv_sem=self.r1.at[side, hop - 1],
            device_id=t.device(sgn, 0), device_id_type=MESH)

    def copy_b(self, d, side, hop):
        t = self.t
        sgn = t.sign_b(d, side)
        iy, ix = t.yx(-d, -sgn * (hop - 1))
        ref = self.buf.at[iy, ix]
        return pltpu.make_async_remote_copy(
            src_ref=ref, dst_ref=ref, send_sem=self.s2.at[side, hop - 1, d + 3], recv_sem=self.r2.at[side, hop - 1, d + 3],
            device_id=t.device(0, sgn), device_id_type=MESH)

    def recv_a(self, side, hop):
        sgn = 1 - 2 * side
        iy, ix = self.t.yx(-sgn * hop, 0)
        ref = self.buf.at[iy, ix]
        pltpu.make_async_remote_copy(
            src_ref=ref, dst_ref=ref, send_sem=self.s1.at[side, hop - 1], recv_sem=self.r1.at[side, hop - 1],
            device_id=self.t.device(-sgn, 0), device_id_type=MESH).wait_recv()

    def recv_b(self, d, side, hop):
        sgn = self.t.sign_b(d, side)
        iy, ix = self.t.yx(-d, -sgn * hop)
        ref = self.buf.at[iy, ix]
        pltpu.make_async_remote_copy(
            src_ref=ref, dst_ref=ref, send_sem=self.s2.at[side, hop - 1, d + 3], recv_sem=self.r2.at[side, hop - 1, d + 3],
            device_id=self.t.device(0, -sgn), device_id_type=MESH).wait_recv()

    def open_column(self, d):
        for side in (0, 1):
            self.copy_b(d, side, 1).start()

    def begin(self):
        self.copy_a(0, 1).start()
        self.copy_a(1, 1).start()
        self.open_column(0)

    def leaf(self, side, hop):
        return hop == self.t.len_b(side)

    def step(self, time):
        t = self.t
        for side in (0, 1):
            if time <= t.len_a(side):
                self.recv_a(side, time)
                if time < t.len_a(side):
                    self.copy_a(side, time + 1).start()
                self.open_column(time if side == 0 else -time)
        for hop in range(1, t.lb + 1):
            dist = time - hop
            if 0 <= dist <= t.la:
                for d in t.offsets(dist):
                    for side in (0, 1):
                        if hop < t.len_b(side):
                            self.recv_b(d, side, hop)
                            self.copy_b(d, side, hop + 1).start()

    def steps(self):
        return self.t.la + self.t.lb

    def all_d(self):
        return [d for dist in range(self.t.la + 1) for d in self.t.offsets(dist)]

    def leaves(self, d):
        for side in (0, 1):
            self.recv_b(d, side, self.t.len_b(side))

    def drain(self):
        for side in (0, 1):
            for hop in range(1, self.t.len_a(side) + 1):
                self.copy_a(side, hop).wait_send()
        for d in self.all_d():
            for side in (0, 1):
                for hop in range(1, self.t.len_b(side) + 1):
                    self.copy_b(d, side, hop).wait_send()


class Scatter:
    def __init__(self, tree, part, out1, in1, out2, in2, s1, r1, s2, r2):
        self.t, self.part = tree, part
        self.out1, self.in1, self.out2, self.in2 = out1, in1, out2, in2
        self.s1, self.r1, self.s2, self.r2 = s1, r1, s2, r2

    def copy_b(self, d, side, hop):
        t = self.t
        sgn = t.sign_b(d, side)
        if hop == t.len_b(side):
            iy, ix = t.yx(-d, -sgn * hop)
            src = self.part.at[iy, ix]
        else:
            src = self.out2.at[side, hop - 1, d + 3]
        return pltpu.make_async_remote_copy(
            src_ref=src, dst_ref=self.in2.at[side, hop - 1, d + 3], send_sem=self.s2.at[side, hop - 1, d + 3],
            recv_sem=self.r2.at[side, hop - 1, d + 3], device_id=t.device(0, -sgn), device_id_type=MESH)

    def copy_a(self, side, hop):
        t = self.t
        sgn = 1 - 2 * side
        return pltpu.make_async_remote_copy(
            src_ref=self.out1.at[side, hop - 1], dst_ref=self.in1.at[side, hop - 1], send_sem=self.s1.at[side, hop - 1],
            recv_sem=self.r1.at[side, hop - 1], device_id=t.device(-sgn, 0), device_id_type=MESH)

    def got_b(self, d, side, hop):
        sgn = self.t.sign_b(d, side)
        ref = self.in2.at[side, hop - 1, d + 3]
        pltpu.make_async_remote_copy(
            src_ref=ref, dst_ref=ref, send_sem=self.s2.at[side, hop - 1, d + 3], recv_sem=self.r2.at[side, hop - 1, d + 3],
            device_id=self.t.device(0, sgn), device_id_type=MESH).wait_recv()
        return ref

    def got_a(self, side, hop):
        sgn = 1 - 2 * side
        ref = self.in1.at[side, hop - 1]
        pltpu.make_async_remote_copy(
            src_ref=ref, dst_ref=ref, send_sem=self.s1.at[side, hop - 1], recv_sem=self.r1.at[side, hop - 1],
            device_id=self.t.device(sgn, 0), device_id_type=MESH).wait_recv()
        return ref

    def send_b(self, d, side, hop):
        t = self.t
        if hop < t.len_b(side):
            got = self.got_b(d, side, hop + 1)
            iy, ix = t.yx(-d, -t.sign_b(d, side) * hop)
            self.out2[side, hop - 1, d + 3] = (self.part[iy, ix].astype(F32) + got[...].astype(F32)).astype(BF16)
        self.copy_b(d, side, hop).start()

    def column_sum(self, d):
        one, two = self.got_b(d, 0, 1), self.got_b(d, 1, 1)
        iy, ix = self.t.yx(-d, 0)
        return self.part[iy, ix].astype(F32) + one[...].astype(F32) + two[...].astype(F32)

    def send_a(self, side, hop):
        t = self.t
        total = self.column_sum(hop if side == 0 else -hop)
        if hop < t.len_a(side):
            total = total + self.got_a(side, hop + 1)[...].astype(F32)
        self.out1[side, hop - 1] = total.astype(BF16)
        self.copy_a(side, hop).start()

    def events(self, depth):
        t = self.t
        leaves, inner = [], []
        for hop in range(t.lb, 0, -1):
            dist = depth - hop
            if 0 <= dist <= t.la:
                for d in t.offsets(dist):
                    for side in (0, 1):
                        if hop == t.len_b(side):
                            leaves.append((d, side, hop))
                        elif hop < t.len_b(side):
                            inner.append((d, side, hop))
        return leaves, inner

    def step(self, depth, ahead=2):
        t = self.t
        top = t.la + t.lb
        depths = range(top, top - ahead - 1, -1) if depth == top else [depth - ahead]
        for later in depths:
            if later >= 1:
                for event in self.events(later)[0]:
                    self.send_b(*event)
        for side in (0, 1):
            if depth <= t.len_a(side):
                self.send_a(side, depth)
        for event in self.events(depth)[1]:
            self.send_b(*event)

    def result(self):
        return self.column_sum(0) + self.got_a(0, 1)[...].astype(F32) + self.got_a(1, 1)[...].astype(F32)

    def drain(self):
        t = self.t
        for side in (0, 1):
            for hop in range(1, t.len_a(side) + 1):
                self.copy_a(side, hop).wait_send()
        for dist in range(t.la + 1):
            for d in t.offsets(dist):
                for side in (0, 1):
                    for hop in range(1, t.len_b(side) + 1):
                        self.copy_b(d, side, hop).wait_send()


def nt_dot(left, right):
    return lax.dot_general(left, right, (((1,), (1,)), ((), ())), preferred_element_type=F32)


def kernel(grad_ref, gate_ref, up_ref, down_ref, gw_ref, uw_ref, in_grad_ref, down_grad_ref,
           rows, hid, part, gu, wcat, rs_out1, rs_in1, rs_out2, rs_in2, hg,
           pair_out, pair_in, z_out, z_in, own,
           h_s1, h_r1, h_s2, h_r2, g_s1, g_r1, g_s2, g_r2, p_s1, p_r1, p_s2, p_r2,
           za_s, za_r, zc_s, zc_r, pair_s, pair_r, zs_s, zs_r):
    row, col = lax.axis_index("row"), lax.axis_index("col")
    z, core = row // 2, lax.rem(row, 2)
    y, x = col // NX, lax.rem(col, NX)
    other = 1 - core
    z_at = lambda off: wrap(z + off, NZ)
    y_at = lambda off: wrap(y + off, NY)
    sibling = (z * 2 + other, col)

    trees = (Tree("y", row, y, x), Tree("x", row, y, x))

    def per_core(fn):
        for which in (0, 1):
            pl.when(core == which)(functools.partial(fn, trees[which]))

    def barrier_partners():
        yield sibling
        for off in range(1, NZ):
            yield (z_at(off) * 2 + core, col)
        for off in (1, -1):
            yield (row, y_at(off) * NX + x)
            yield (row, y * NX + wrap(x + off, NX))

    barrier = pltpu.get_barrier_semaphore()
    count = 0
    for partner in barrier_partners():
        pl.semaphore_signal(barrier, inc=1, device_id=partner, device_id_type=MESH)
        count += 1

    gate = gate_ref[...].astype(F32)
    sig = jax.nn.sigmoid(gate)
    hid[y, x] = (gate * sig * up_ref[...].astype(F32)).astype(BF16)
    rows[row] = grad_ref[...]
    pl.semaphore_wait(barrier, count)

    def z_copy(side, hop):
        sgn = 1 - 2 * side
        ref = rows.at[z_at(-sgn * (hop - 1)) * 2 + core]
        return pltpu.make_async_remote_copy(
            src_ref=ref, dst_ref=ref, send_sem=za_s.at[side, hop - 1], recv_sem=za_r.at[side, hop - 1],
            device_id=(z_at(sgn) * 2 + core, col), device_id_type=MESH)

    def z_recv(side, hop):
        sgn = 1 - 2 * side
        ref = rows.at[z_at(-sgn * hop) * 2 + core]
        pltpu.make_async_remote_copy(
            src_ref=ref, dst_ref=ref, send_sem=za_s.at[side, hop - 1], recv_sem=za_r.at[side, hop - 1],
            device_id=(z_at(-sgn) * 2 + core, col), device_id_type=MESH).wait_recv()

    def cross_copy(off, which):
        ref = rows.at[z_at(off) * 2 + which]
        return pltpu.make_async_remote_copy(
            src_ref=ref, dst_ref=ref, send_sem=zc_s.at[off + 3], recv_sem=zc_r.at[off + 3],
            device_id=sibling, device_id_type=MESH)

    def hidden_gather(tree):
        return Gather(tree, hid, h_s1, h_r1, h_s2, h_r2)

    def grads_gather(tree):
        return Gather(tree, gu, g_s1, g_r1, g_s2, g_r2)

    def scatter(tree):
        return Scatter(tree, part, rs_out1, rs_in1, rs_out2, rs_in2, p_s1, p_r1, p_s2, p_r2)

    z_copy(0, 1).start()
    z_copy(1, 1).start()
    per_core(lambda tree: hidden_gather(tree).begin())
    cross_copy(0, core).start()
    wcat[:, :HEAD] = gw_ref[:, :HEAD]
    wcat[:, HEAD:2 * HEAD] = uw_ref[:, :HEAD]
    wcat[:, 2 * HEAD:] = jnp.concatenate([gw_ref[:, HEAD:], uw_ref[:, HEAD:]], axis=1)

    def matmul1(off):
        iz = z_at(off)
        block = rows[pl.ds(iz * 2, 2)].reshape(2 * PAIR, FEAT)
        part[iz] = nt_dot(block, down_ref[...]).astype(BF16).reshape(NX, TOK, UNITS)

    for hop in range(1, NZ // 2 + 1):
        for side in (0, 1):
            if hop <= NZ // 2 - side:
                z_recv(side, hop)
                if hop < NZ // 2 - side:
                    z_copy(side, hop + 1).start()
                cross_copy(-hop if side == 0 and hop < 4 else hop, core).start()
        per_core(lambda tree: hidden_gather(tree).step(hop))
    offs = [0, -1, 1, -2, 2, -3, 3, 4]
    for off in offs:
        cross_copy(off, other).wait_recv()
        matmul1(off)
    for time in (5, 6):
        per_core(lambda tree: hidden_gather(tree).step(time))

    for depth in range(6, 0, -1):
        per_core(lambda tree: scatter(tree).step(depth))

    def finish(tree):
        hg[...] = scatter(tree).result()

    per_core(finish)
    grad = hg[...]
    upv = up_ref[...].astype(F32)
    ug = (grad * (gate * sig)).astype(BF16)
    gg = (grad * upv * sig * (1.0 + gate * (1.0 - sig))).astype(BF16)
    gu[y, x, :, :HEAD] = gg[:, :HEAD]
    gu[y, x, :, HEAD:2 * HEAD] = ug[:, :HEAD]
    gu[y, x, :, 2 * HEAD:] = jnp.concatenate([gg[:, HEAD:], ug[:, HEAD:]], axis=1)

    per_core(lambda tree: grads_gather(tree).begin())

    def hidden_leaves(tree):
        gather = hidden_gather(tree)
        for d in gather.all_d():
            gather.leaves(d)

    per_core(hidden_leaves)
    all_rows = rows[...].reshape(NZ * 2 * PAIR, FEAT)
    for start, size in ((0, 256), (256, 256), (512, 320)):
        units = hid[:, :, :, pl.ds(start, size)].reshape(NY * NX * TOK, size)
        down_grad_ref[pl.ds(start, size)] = lax.dot_general(
            units, all_rows, (((0,), (0,)), ((), ())), preferred_element_type=F32).astype(BF16)

    def pair_copy(off):
        return pltpu.make_async_remote_copy(
            src_ref=pair_out.at[off + 3], dst_ref=pair_in.at[off + 3], send_sem=pair_s.at[off + 3],
            recv_sem=pair_r.at[off + 3], device_id=sibling, device_id_type=MESH)

    def z_send(off):
        return pltpu.make_async_remote_copy(
            src_ref=z_out.at[off + 3], dst_ref=z_in.at[z], send_sem=zs_s.at[off + 3], recv_sem=zs_r.at[z],
            device_id=(y_at(off) * 2 + core, col), device_id_type=MESH)

    def block_leaves(tree, off):
        gather = grads_gather(tree)
        if tree.first == "y":
            gather.leaves(-off if off != 4 else 4)
        else:
            for d in gather.all_d():
                for side in (0, 1):
                    sgn = tree.sign_b(d, side)
                    hop = abs(off)
                    if hop == tree.len_b(side) and (-sgn * hop - off) % NY == 0:
                        gather.recv_b(d, side, hop)

    def block(off):
        per_core(lambda tree: block_leaves(tree, off))
        iy = y_at(off)
        both = gu[iy].reshape(NX * TOK, WIDE)
        total = nt_dot(both, wcat[...])
        lower, upper = total[:PAIR], total[PAIR:]
        mine = jnp.where(core == 0, lower, upper)
        theirs = jnp.where(core == 0, upper, lower)
        pair_out[off + 3] = theirs.astype(BF16)
        own[off + 3] = mine
        pair_copy(off).start()

    def pass_on(off):
        pair_copy(off).wait_recv()
        total = own[off + 3] + pair_in[off + 3].astype(F32)
        own[off + 3] = total

        @pl.when(y_at(off) != z)
        def _():
            z_out[off + 3] = total.astype(BF16)
            z_send(off).start()

        @pl.when(y_at(off) == z)
        def _():
            own[8] = total

    done = []

    def run_block(off):
        block(off)
        if done:
            pass_on(done[-1])
        done.append(off)

    for time in range(1, 7):
        per_core(lambda tree: grads_gather(tree).step(time))
        dist = time - 3
        if dist >= 0:
            for off in ([0] if dist == 0 else [dist, -dist]):
                run_block(off)
    run_block(4)
    pass_on(4)

    total = own[8]
    for off in range(1, NZ):
        iz = z_at(off)
        ref = z_in.at[iz]
        pltpu.make_async_remote_copy(
            src_ref=ref, dst_ref=ref, send_sem=zs_s.at[0], recv_sem=zs_r.at[iz],
            device_id=(iz * 2 + core, col), device_id_type=MESH).wait_recv()
        total = total + ref[...].astype(F32)
    in_grad_ref[...] = total.astype(BF16)

    for side in (0, 1):
        for hop in range(1, NZ // 2 + 1 - side):
            z_copy(side, hop).wait_send()
    for off in range(-3, 5):
        cross_copy(off, core).wait_send()
        pair_copy(off).wait_send()
        pl.when(y_at(off) != z)(lambda: z_send(off).wait_send())

    def drain(tree):
        hidden_gather(tree).drain()
        scatter(tree).drain()
        grads_gather(tree).drain()

    per_core(drain)


def on_device(grad_out, gate_pre, up_pre, down_weight, gate_weight, up_weight):
    vmem = pl.BlockSpec(memory_space=pltpu.VMEM)
    dma = pltpu.SemaphoreType.DMA
    tree_sems = [dma((2, 4)), dma((2, 4)), dma((2, 4, 8)), dma((2, 4, 8))]
    return pl.pallas_call(
        kernel,
        out_shape=(
            jax.ShapeDtypeStruct((PAIR, FEAT), BF16),
            jax.ShapeDtypeStruct((UNITS, FEAT), BF16),
        ),
        in_specs=[vmem] * 6,
        out_specs=(vmem, vmem),
        scratch_shapes=[
            pltpu.VMEM((2 * NZ, PAIR, FEAT), BF16),
            pltpu.VMEM((NY, NX, TOK, UNITS), BF16),
            pltpu.VMEM((NY, NX, TOK, UNITS), BF16),
            pltpu.VMEM((NY, NX, TOK, WIDE), BF16),
            pltpu.VMEM((FEAT, WIDE), BF16),
            pltpu.VMEM((2, 4, TOK, UNITS), BF16),
            pltpu.VMEM((2, 4, TOK, UNITS), BF16),
            pltpu.VMEM((2, 4, 8, TOK, UNITS), BF16),
            pltpu.VMEM((2, 4, 8, TOK, UNITS), BF16),
            pltpu.VMEM((TOK, UNITS), F32),
            pltpu.VMEM((8, PAIR, FEAT), BF16),
            pltpu.VMEM((8, PAIR, FEAT), BF16),
            pltpu.VMEM((8, PAIR, FEAT), BF16),
            pltpu.VMEM((8, PAIR, FEAT), BF16),
            pltpu.VMEM((9, PAIR, FEAT), F32),
        ] + tree_sems * 3 + [dma((2, 4)), dma((2, 4))] + [dma((8,))] * 6,
        compiler_params=pltpu.CompilerParams(
            collective_id=0, has_side_effects=True, vmem_limit_bytes=56 * 2**20),
        cost_estimate=pl.CostEstimate(flops=5_234_491_392, bytes_accessed=4_000_000, transcendentals=40_000),
    )(grad_out, gate_pre, up_pre, down_weight, gate_weight, up_weight)


def solution(mesh):
    placed = (
        P("row", "col"),
        P("col", "row"),
        P("col", "row"),
        P("row", "col"),
        P("col", "row"),
        P("col", "row"),
    )
    return jax.shard_map(
        on_device,
        mesh=mesh,
        in_specs=placed,
        out_specs=(P("row", "col"), P("row", "col")),
        check_vma=False,
    )
```

```python
import functools

import jax
import jax.numpy as jnp
from jax import lax
from jax.experimental import pallas as pl
from jax.experimental.pallas import tpu as pltpu
from jax.sharding import PartitionSpec as P

NZ, NY, NX = 8, 8, 4
TOK = 48
PAIR = 96
UNITS = 832
WIDE = 2 * UNITS
HEAD = 768
FEAT = 512
MESH = pl.DeviceIdType.MESH
F32, BF16 = jnp.float32, jnp.bfloat16


def wrap(value, size):
    return lax.rem(value + 2 * size, size)


class Torus:
    def __init__(self, row, y, x):
        self.row, self.y, self.x = row, y, x

    def yx(self, off_y, off_x):
        return wrap(self.y + off_y, NY), wrap(self.x + off_x, NX)

    def device(self, off_y, off_x):
        iy, ix = self.yx(off_y, off_x)
        return (self.row, iy * NX + ix)


LONG = NY // 2
HOPS = (LONG, LONG - 1)
DIRECT = (2, 1, -1)
COLUMNS = (0, 1, -1, 2)


def y_offsets(dist):
    return [dist] if dist in (0, LONG) else [dist, -dist]


FAR_FIRST = [d for dist in range(LONG, -1, -1) for d in y_offsets(dist)]


def sign(d, side):
    return 1 - 2 * ((d + side) % 2)


def chain_slot(d, side, hop):
    return (side * LONG + hop - 1) * 4 + d + 1


def direct_slot(d, e):
    return DIRECT.index(e) * 8 + d + 3


def remote(src, dst, send, recv, device):
    return pltpu.make_async_remote_copy(
        src_ref=src, dst_ref=dst, send_sem=send, recv_sem=recv, device_id=device, device_id_type=MESH)


class GatherYX:
    def __init__(self, t, buf, s1, r1, s2, r2):
        self.t, self.buf, self.s1, self.r1, self.s2, self.r2 = t, buf, s1, r1, s2, r2

    def ref(self, off_y, off_x):
        return self.buf.at[self.t.yx(off_y, off_x)]

    def copy_y(self, side, hop, to=0):
        sgn = 1 - 2 * side
        ref = self.ref(-sgn * (hop - 1 + to), 0)
        slot = side * LONG + hop - 1
        return remote(ref, ref, self.s1.at[slot], self.r1.at[slot], self.t.device(sgn, 0))

    def copy_x(self, d, e, to=0):
        ref = self.ref(-d, -e * to)
        slot = direct_slot(d, e)
        return remote(ref, ref, self.s2.at[slot], self.r2.at[slot], self.t.device(0, e))

    def open(self, d):
        for e in DIRECT:
            self.copy_x(d, e).start()

    def begin(self):
        for side in (0, 1):
            self.copy_y(side, 1).start()
        self.open(0)

    def step(self, time):
        for side in (0, 1):
            if time <= HOPS[side]:
                self.copy_y(side, time, 1).wait_recv()
                if time < HOPS[side]:
                    self.copy_y(side, time + 1).start()
        for side in (0, 1):
            if time <= HOPS[side]:
                self.open(time if side == 0 else -time)

    def leaves(self, off):
        for e in DIRECT:
            self.copy_x(off if off == LONG else -off, e, 1).wait_recv()

    def drain(self):
        for side in (0, 1):
            for hop in range(1, HOPS[side] + 1):
                self.copy_y(side, hop).wait_send()
        for d in FAR_FIRST:
            for e in DIRECT:
                self.copy_x(d, e).wait_send()


class GatherXY:
    def __init__(self, t, buf, s1, r1, s2, r2):
        self.t, self.buf, self.s1, self.r1, self.s2, self.r2 = t, buf, s1, r1, s2, r2

    def ref(self, off_y, off_x):
        return self.buf.at[self.t.yx(off_y, off_x)]

    def copy_x(self, e, to=0):
        ref = self.ref(0, -e * to)
        slot = DIRECT.index(e)
        return remote(ref, ref, self.s1.at[slot], self.r1.at[slot], self.t.device(0, e))

    def copy_y(self, d, side, hop, to=0):
        sgn = sign(d, side)
        ref = self.ref(-sgn * (hop - 1 + to), -d)
        slot = chain_slot(d, side, hop)
        return remote(ref, ref, self.s2.at[slot], self.r2.at[slot], self.t.device(sgn, 0))

    def begin(self):
        for e in DIRECT:
            self.copy_x(e).start()
        for side in (0, 1):
            self.copy_y(0, side, 1).start()

    def step(self, time):
        if time == 1:
            for e in (1, -1, 2):
                self.copy_x(e, 1).wait_recv()
                for side in (0, 1):
                    self.copy_y(e, side, 1).start()
        for d in COLUMNS:
            hop = time if d == 0 else time - 1
            for side in (0, 1):
                if 1 <= hop < HOPS[side]:
                    self.copy_y(d, side, hop, 1).wait_recv()
                    self.copy_y(d, side, hop + 1).start()

    def leaves(self, off):
        for d in COLUMNS:
            for side in (0, 1):
                hop = HOPS[side]
                if hop == abs(off) and (-sign(d, side) * hop - off) % NY == 0:
                    self.copy_y(d, side, hop, 1).wait_recv()

    def drain(self):
        for e in DIRECT:
            self.copy_x(e).wait_send()
        for d in COLUMNS:
            for side in (0, 1):
                for hop in range(1, HOPS[side] + 1):
                    self.copy_y(d, side, hop).wait_send()


class ScatterYX:
    def __init__(self, t, part, out1, in1, out2, in2, s1, r1, s2, r2):
        self.t, self.part, self.out1, self.in1, self.in2 = t, part, out1, in1, in2
        self.s1, self.r1, self.s2, self.r2 = s1, r1, s2, r2

    def copy_x(self, d, e):
        slot = direct_slot(d, e)
        return remote(self.part.at[self.t.yx(-d, -e)], self.in2.at[slot], self.s2.at[slot], self.r2.at[slot],
                      self.t.device(0, -e))

    def copy_y(self, side, hop):
        slot = side * LONG + hop - 1
        return remote(self.out1.at[slot], self.in1.at[slot], self.s1.at[slot], self.r1.at[slot],
                      self.t.device(-1 + 2 * side, 0))

    def open(self, d):
        for e in DIRECT:
            self.copy_x(d, e).start()

    def column_sum(self, d):
        total = self.part[self.t.yx(-d, 0)].astype(F32)
        for e in DIRECT:
            self.copy_x(d, e).wait_recv()
            total = total + self.in2[direct_slot(d, e)].astype(F32)
        return total

    def got_y(self, side, hop):
        self.copy_y(side, hop).wait_recv()
        return self.in1[side * LONG + hop - 1].astype(F32)

    def step(self, depth):
        for side in (0, 1):
            if depth <= HOPS[side]:
                total = self.column_sum(depth if side == 0 else -depth)
                if depth < HOPS[side]:
                    total = total + self.got_y(side, depth + 1)
                self.out1[side * LONG + depth - 1] = total.astype(BF16)
                self.copy_y(side, depth).start()

    def result(self):
        return self.column_sum(0) + self.got_y(0, 1) + self.got_y(1, 1)

    def drain(self):
        for side in (0, 1):
            for hop in range(1, HOPS[side] + 1):
                self.copy_y(side, hop).wait_send()
        for d in FAR_FIRST:
            for e in DIRECT:
                self.copy_x(d, e).wait_send()


class ScatterXY:
    def __init__(self, t, part, out1, in1, out2, in2, s1, r1, s2, r2):
        self.t, self.part, self.out1, self.in1, self.out2, self.in2 = t, part, out1, in1, out2, in2
        self.s1, self.r1, self.s2, self.r2 = s1, r1, s2, r2

    def copy_y(self, d, side, hop):
        sgn = sign(d, side)
        slot = chain_slot(d, side, hop)
        if hop == HOPS[side]:
            src = self.part.at[self.t.yx(-sgn * hop, -d)]
        else:
            src = self.out2.at[slot]
        return remote(src, self.in2.at[slot], self.s2.at[slot], self.r2.at[slot], self.t.device(-sgn, 0))

    def copy_x(self, e):
        slot = DIRECT.index(e)
        return remote(self.out1.at[slot], self.in1.at[slot], self.s1.at[slot], self.r1.at[slot], self.t.device(0, -e))

    def open(self, off):
        for d in (2, 1, -1, 0):
            for side in (0, 1):
                if HOPS[side] == abs(off) and (sign(d, side) * HOPS[side] - off) % NY == 0:
                    self.copy_y(d, side, HOPS[side]).start()

    def got_y(self, d, side, hop):
        self.copy_y(d, side, hop).wait_recv()
        return self.in2[chain_slot(d, side, hop)].astype(F32)

    def column_sum(self, d):
        return self.part[self.t.yx(0, -d)].astype(F32) + self.got_y(d, 0, 1) + self.got_y(d, 1, 1)

    def step(self, depth):
        for d in (2, 1, -1, 0):
            for side in (0, 1):
                hop = depth - 1
                if 1 <= hop < HOPS[side]:
                    total = self.part[self.t.yx(-sign(d, side) * hop, -d)].astype(F32) + self.got_y(d, side, hop + 1)
                    self.out2[chain_slot(d, side, hop)] = total.astype(BF16)
                    self.copy_y(d, side, hop).start()
            if depth == 1 and d != 0:
                self.out1[DIRECT.index(d)] = self.column_sum(d).astype(BF16)
                self.copy_x(d).start()

    def result(self):
        total = self.column_sum(0)
        for e in DIRECT:
            self.copy_x(e).wait_recv()
            total = total + self.in1[DIRECT.index(e)].astype(F32)
        return total

    def drain(self):
        for e in DIRECT:
            self.copy_x(e).wait_send()
        for d in COLUMNS:
            for side in (0, 1):
                for hop in range(1, HOPS[side] + 1):
                    self.copy_y(d, side, hop).wait_send()


def nt_dot(left, right):
    return lax.dot_general(left, right, (((1,), (1,)), ((), ())), preferred_element_type=F32)


def kernel(grad_ref, gate_ref, up_ref, down_hbm, gw_hbm, uw_hbm, in_grad_ref, down_grad_ref,
           rows, hid, part, gu, down_ref, wcat, rs_out1, rs_in1, rs_out2, rs_in2, hg,
           pair_out, pair_in, z_out, z_in, own,
           h_s1, h_r1, h_s2, h_r2, g_s1, g_r1, g_s2, g_r2, p_s1, p_r1, p_s2, p_r2,
           za_s, za_r, zc_s, zc_r, pair_s, pair_r, zs_s, zs_r, load_sem):
    row, col = lax.axis_index("row"), lax.axis_index("col")
    z, core = row // 2, lax.rem(row, 2)
    y, x = col // NX, lax.rem(col, NX)
    other = 1 - core
    way = 1 - 2 * core
    z_at = lambda off: wrap(z + off, NZ)
    y_at = lambda off: wrap(y + off, NY)
    sibling = (z * 2 + other, col)
    torus = Torus(row, y, x)

    def per_core(fn):
        for which in (0, 1):
            pl.when(core == which)(functools.partial(fn, which))

    partners = [sibling]
    partners += [(z_at(off) * 2 + core, col) for off in range(1, NZ)]
    partners += [torus.device(1, 0), torus.device(-1, 0)] + [torus.device(0, e) for e in DIRECT]
    barrier = pltpu.get_barrier_semaphore()
    for partner in partners:
        pl.semaphore_signal(barrier, inc=1, device_id=partner, device_id_type=MESH)

    loads = [pltpu.make_async_copy(down_hbm, down_ref, load_sem.at[0])]
    for i, (src, size, at) in enumerate(((gw_hbm, HEAD, 0), (uw_hbm, HEAD, HEAD))):
        loads.append(pltpu.make_async_copy(src.at[pl.ds(0, size)], wcat.at[pl.ds(at, size)], load_sem.at[1 + 2 * i]))
        loads.append(pltpu.make_async_copy(
            src.at[pl.ds(HEAD, UNITS - HEAD)], wcat.at[pl.ds(2 * HEAD + i * (UNITS - HEAD), UNITS - HEAD)],
            load_sem.at[2 + 2 * i]))
    for load in loads:
        load.start()

    gate = gate_ref[...].astype(F32)
    sig = jax.nn.sigmoid(gate)
    hid[y, x] = (gate * sig * up_ref[...].astype(F32)).astype(BF16)
    rows[row] = grad_ref[...]
    pl.semaphore_wait(barrier, len(partners))

    def z_copy(off, via=0, to=0):
        ref = rows.at[z_at(-way * (off if to else via)) * 2 + core]
        slot = off + 3
        return remote(ref, ref, za_s.at[slot], za_r.at[slot], (z_at(way * (off - via)) * 2 + core, col))

    def cross_copy(off, which):
        ref = rows.at[z_at(off) * 2 + which]
        return remote(ref, ref, zc_s.at[off + 3], zc_r.at[off + 3], sibling)

    def cross_slot(off, sgn):
        return 4 if abs(off) == 4 else off * sgn

    def hidden_gather(which):
        return (GatherYX, GatherXY)[which](torus, hid, h_s1, h_r1, h_s2, h_r2)

    def grads_gather(which):
        return (GatherYX, GatherXY)[which](torus, gu, g_s1, g_r1, g_s2, g_r2)

    def scatter(which):
        return (ScatterYX, ScatterXY)[which](torus, part, rs_out1, rs_in1, rs_out2, rs_in2, p_s1, p_r1, p_s2, p_r2)

    def z_got(off):
        z_copy(off, 0, 1).wait_recv()

    def z_pass(off):
        def send(which):
            cross_copy(cross_slot(-off, 1 - 2 * which), which).start()

        per_core(send)

    for off in (2, -2, 1, -1):
        z_copy(off).start()
    per_core(lambda which: hidden_gather(which).begin())
    cross_copy(0, core).start()
    z_got(2)
    z_copy(4, 2).start()
    z_copy(3, 2).start()
    z_got(-2)
    z_copy(-3, -2).start()
    for off in (2, -2):
        z_pass(off)
    for off in (1, -1):
        z_got(off)
        z_pass(off)
    for time in (1, 2):
        per_core(lambda which: hidden_gather(which).step(time))
    for off in (3, -3, 4):
        z_got(off)
        z_pass(off)
    for load in loads:
        load.wait()
    for off in range(-3, 5):
        cross_copy(off, other).wait_recv()

    def matmul1(off):
        iz = y_at(off)
        block = rows[pl.ds(iz * 2, 2)].reshape(2 * PAIR, FEAT)
        part[iz] = nt_dot(block, down_ref[...]).astype(BF16).reshape(NX, TOK, UNITS)

    for off in FAR_FIRST:
        matmul1(-off)
        per_core(lambda which: scatter(which).open(off))
    for depth in (4, 3, 2, 1):
        per_core(lambda which: scatter(which).step(depth))

    def finish(which):
        hg[...] = scatter(which).result()

    per_core(finish)
    grad = hg[...]
    upv = up_ref[...].astype(F32)
    ug = (grad * (gate * sig)).astype(BF16)
    gg = (grad * upv * sig * (1.0 + gate * (1.0 - sig))).astype(BF16)
    gu[y, x, :, :HEAD] = gg[:, :HEAD]
    gu[y, x, :, HEAD:2 * HEAD] = ug[:, :HEAD]
    gu[y, x, :, 2 * HEAD:] = jnp.concatenate([gg[:, HEAD:], ug[:, HEAD:]], axis=1)

    per_core(lambda which: grads_gather(which).begin())

    def pair_copy(off):
        slot = off + 3
        return remote(pair_out.at[slot], pair_in.at[slot], pair_s.at[slot], pair_r.at[slot], sibling)

    def z_send(off):
        return remote(z_out.at[off + 3], z_in.at[z], zs_s.at[off + 3], zs_r.at[z], (y_at(off) * 2 + core, col))

    def block(off):
        per_core(lambda which: grads_gather(which).leaves(off))
        both = gu[y_at(off)].reshape(NX * TOK, WIDE)
        total = jnp.dot(both, wcat[...], preferred_element_type=F32)
        lower, upper = total[:PAIR], total[PAIR:]
        own[off + 3] = jnp.where(core == 0, lower, upper)
        pair_out[off + 3] = jnp.where(core == 0, upper, lower).astype(BF16)
        pair_copy(off).start()

    def pass_on(off):
        pair_copy(off).wait_recv()
        total = own[off + 3] + pair_in[off + 3].astype(F32)

        @pl.when(y_at(off) != z)
        def _():
            z_out[off + 3] = total.astype(BF16)
            z_send(off).start()

        @pl.when(y_at(off) == z)
        def _():
            own[8] = total

    for time in (1, 2, 3, 4):
        per_core(lambda which: grads_gather(which).step(time))
        if time == 2:
            block(0)
        if time == 3:
            pass_on(0)
            block(1)
            block(-1)
    pass_on(1)
    pass_on(-1)
    for time in (3, 4):
        per_core(lambda which: hidden_gather(which).step(time))
    for off in (2, -2):
        block(off)
    for off in (2, -2):
        pass_on(off)
    for off in (3, -3):
        block(off)
    for off in (3, -3):
        pass_on(off)
    block(4)
    pass_on(4)

    def hidden_leaves(which):
        for off in FAR_FIRST:
            hidden_gather(which).leaves(off)

    per_core(hidden_leaves)
    all_rows = rows[...].reshape(NZ * 2 * PAIR, FEAT)
    for start, size in ((0, 256), (256, 256), (512, 320)):
        units = hid[:, :, :, pl.ds(start, size)].reshape(NY * NX * TOK, size)
        down_grad_ref[pl.ds(start, size)] = lax.dot_general(
            units, all_rows, (((0,), (0,)), ((), ())), preferred_element_type=F32).astype(BF16)

    total = own[8]
    for off in range(1, NZ):
        iz = z_at(off)
        ref = z_in.at[iz]
        remote(ref, ref, zs_s.at[0], zs_r.at[iz], (iz * 2 + core, col)).wait_recv()
        total = total + ref[...].astype(F32)
    in_grad_ref[...] = total.astype(BF16)

    for off, via in ((2, 0), (-2, 0), (1, 0), (-1, 0), (4, 2), (3, 2), (-3, -2)):
        z_copy(off, via).wait_send()
    for off in range(-3, 5):
        cross_copy(off, core).wait_send()
        pair_copy(off).wait_send()
        pl.when(y_at(off) != z)(lambda: z_send(off).wait_send())

    def drain(which):
        hidden_gather(which).drain()
        scatter(which).drain()
        grads_gather(which).drain()

    per_core(drain)


def copy_out(a_ref, b_ref, a_out, b_out):
    a_out[...] = a_ref[...]
    b_out[...] = b_ref[...]


def on_device(grad_out, gate_pre, up_pre, down_weight, gate_weight, up_weight):
    vmem, anywhere = pl.BlockSpec(memory_space=pltpu.VMEM), pl.BlockSpec(memory_space=pl.ANY)
    dma = pltpu.SemaphoreType.DMA
    tree_sems = [dma((8,)), dma((8,)), dma((32,)), dma((32,))]
    outs = (jax.ShapeDtypeStruct((PAIR, FEAT), BF16), jax.ShapeDtypeStruct((UNITS, FEAT), BF16))
    input_grad, down_grad = pl.pallas_call(
        kernel,
        out_shape=outs,
        in_specs=[vmem] * 3 + [anywhere] * 3,
        out_specs=(vmem, vmem),
        scratch_shapes=[
            pltpu.VMEM((2 * NZ, PAIR, FEAT), BF16),
            pltpu.VMEM((NY, NX, TOK, UNITS), BF16),
            pltpu.VMEM((NY, NX, TOK, UNITS), BF16),
            pltpu.VMEM((NY, NX, TOK, WIDE), BF16),
            pltpu.VMEM((UNITS, FEAT), BF16),
            pltpu.VMEM((WIDE, FEAT), BF16),
            pltpu.VMEM((8, TOK, UNITS), BF16),
            pltpu.VMEM((8, TOK, UNITS), BF16),
            pltpu.VMEM((32, TOK, UNITS), BF16),
            pltpu.VMEM((32, TOK, UNITS), BF16),
            pltpu.VMEM((TOK, UNITS), F32),
            pltpu.VMEM((8, PAIR, FEAT), BF16),
            pltpu.VMEM((8, PAIR, FEAT), BF16),
            pltpu.VMEM((8, PAIR, FEAT), BF16),
            pltpu.VMEM((8, PAIR, FEAT), BF16),
            pltpu.VMEM((9, PAIR, FEAT), F32),
        ] + tree_sems * 3 + [dma((8,))] * 8 + [dma((5,))],
        compiler_params=pltpu.CompilerParams(
            collective_id=0, has_side_effects=True, vmem_limit_bytes=56 * 2**20),
        cost_estimate=pl.CostEstimate(flops=5_234_491_392, bytes_accessed=4_000_000, transcendentals=40_000),
    )(grad_out, gate_pre, up_pre, down_weight, gate_weight.T, up_weight.T)
    return pl.pallas_call(
        copy_out,
        out_shape=outs,
        in_specs=[vmem] * 2,
        out_specs=(vmem, vmem),
    )(input_grad, down_grad)


def solution(mesh):
    placed = (
        P("row", "col"),
        P("col", "row"),
        P("col", "row"),
        P("row", "col"),
        P("col", "row"),
        P("col", "row"),
    )
    return jax.shard_map(
        on_device,
        mesh=mesh,
        in_specs=placed,
        out_specs=(P("row", "col"), P("row", "col")),
        check_vma=False,
    )
```

```python
import functools

import jax
import jax.numpy as jnp
from jax import lax
from jax.experimental import pallas as pl
from jax.experimental.pallas import tpu as pltpu
from jax.sharding import PartitionSpec as P

NZ, NY, NX = 8, 8, 4
TOK = 48
PAIR = 96
UNITS = 832
WIDE = 2 * UNITS
HEAD = 768
FEAT = 512
MESH = pl.DeviceIdType.MESH
F32, BF16 = jnp.float32, jnp.bfloat16


def wrap(value, size):
    return lax.rem(value + 2 * size, size)


class Torus:
    def __init__(self, row, y, x):
        self.row, self.y, self.x = row, y, x

    def yx(self, off_y, off_x):
        return wrap(self.y + off_y, NY), wrap(self.x + off_x, NX)

    def device(self, off_y, off_x):
        iy, ix = self.yx(off_y, off_x)
        return (self.row, iy * NX + ix)


LONG = NY // 2
HOPS = (LONG, LONG - 1)
DIRECT = (2, 1, -1)
AFTER = {4: 3, 1: 4}
COLUMNS = (0, 1, -1, 2)


def y_offsets(dist):
    return [dist] if dist in (0, LONG) else [dist, -dist]


FAR_FIRST = [d for dist in range(LONG, -1, -1) for d in y_offsets(dist)]


def sign(d, side):
    return 1 - 2 * ((d + side) % 2)


def chain_slot(d, side, hop):
    return (side * LONG + hop - 1) * 4 + d + 1


def direct_slot(d, e):
    return DIRECT.index(e) * 8 + d + 3


def remote(src, dst, send, recv, device):
    return pltpu.make_async_remote_copy(
        src_ref=src, dst_ref=dst, send_sem=send, recv_sem=recv, device_id=device, device_id_type=MESH)


class GatherYX:
    def __init__(self, t, buf, s1, r1, s2, r2):
        self.t, self.buf, self.s1, self.r1, self.s2, self.r2 = t, buf, s1, r1, s2, r2

    def ref(self, off_y, off_x):
        return self.buf.at[self.t.yx(off_y, off_x)]

    def copy_y(self, side, hop, to=0):
        sgn = 1 - 2 * side
        ref = self.ref(-sgn * (hop - 1 + to), 0)
        slot = side * LONG + hop - 1
        return remote(ref, ref, self.s1.at[slot], self.r1.at[slot], self.t.device(sgn, 0))

    def copy_x(self, d, e, to=0):
        ref = self.ref(-d, -e * to)
        slot = direct_slot(d, e)
        return remote(ref, ref, self.s2.at[slot], self.r2.at[slot], self.t.device(0, e))

    def open(self, d):
        for e in DIRECT:
            self.copy_x(d, e).start()

    def begin(self):
        for side in (0, 1):
            self.copy_y(side, 1).start()
        self.open(0)

    def step(self, time):
        for side in (0, 1):
            if time <= HOPS[side]:
                self.copy_y(side, time, 1).wait_recv()
                if time < HOPS[side]:
                    self.copy_y(side, time + 1).start()
        for side in (0, 1):
            if time <= HOPS[side]:
                self.open(time if side == 0 else -time)

    def leaves(self, off):
        for e in DIRECT:
            self.copy_x(off if off == LONG else -off, e, 1).wait_recv()

    def drain(self):
        for side in (0, 1):
            for hop in range(1, HOPS[side] + 1):
                self.copy_y(side, hop).wait_send()
        for d in FAR_FIRST:
            for e in DIRECT:
                self.copy_x(d, e).wait_send()


class GatherXY:
    def __init__(self, t, buf, s1, r1, s2, r2):
        self.t, self.buf, self.s1, self.r1, self.s2, self.r2 = t, buf, s1, r1, s2, r2

    def ref(self, off_y, off_x):
        return self.buf.at[self.t.yx(off_y, off_x)]

    def copy_x(self, e, to=0):
        ref = self.ref(0, -e * to)
        slot = DIRECT.index(e)
        return remote(ref, ref, self.s1.at[slot], self.r1.at[slot], self.t.device(0, e))

    def copy_y(self, d, side, hop, to=0):
        sgn = sign(d, side)
        ref = self.ref(-sgn * (hop - 1 + to), -d)
        slot = chain_slot(d, side, hop)
        return remote(ref, ref, self.s2.at[slot], self.r2.at[slot], self.t.device(sgn, 0))

    def begin(self):
        for e in DIRECT:
            self.copy_x(e).start()
        for side in (0, 1):
            self.copy_y(0, side, 1).start()

    def step(self, time):
        if time == 1:
            for e in (1, -1, 2):
                self.copy_x(e, 1).wait_recv()
                for side in (0, 1):
                    self.copy_y(e, side, 1).start()
        for d in COLUMNS:
            hop = time if d == 0 else time - 1
            for side in (0, 1):
                if 1 <= hop < HOPS[side]:
                    self.copy_y(d, side, hop, 1).wait_recv()
                    self.copy_y(d, side, hop + 1).start()

    def leaves(self, off):
        for d in COLUMNS:
            for side in (0, 1):
                hop = HOPS[side]
                if hop == abs(off) and (-sign(d, side) * hop - off) % NY == 0:
                    self.copy_y(d, side, hop, 1).wait_recv()

    def drain(self):
        for e in DIRECT:
            self.copy_x(e).wait_send()
        for d in COLUMNS:
            for side in (0, 1):
                for hop in range(1, HOPS[side] + 1):
                    self.copy_y(d, side, hop).wait_send()


class ScatterYX:
    def __init__(self, t, part, out1, in1, out2, in2, s1, r1, s2, r2):
        self.t, self.part, self.out1, self.in1, self.in2 = t, part, out1, in1, in2
        self.s1, self.r1, self.s2, self.r2 = s1, r1, s2, r2

    def copy_x(self, d, e):
        slot = direct_slot(d, e)
        return remote(self.part.at[self.t.yx(-d, -e)], self.in2.at[slot], self.s2.at[slot], self.r2.at[slot],
                      self.t.device(0, -e))

    def copy_y(self, side, hop):
        slot = side * LONG + hop - 1
        return remote(self.out1.at[slot], self.in1.at[slot], self.s1.at[slot], self.r1.at[slot],
                      self.t.device(-1 + 2 * side, 0))

    def open(self, d):
        for e in DIRECT:
            self.copy_x(d, e).start()

    def column_sum(self, d):
        total = self.part[self.t.yx(-d, 0)].astype(F32)
        for e in DIRECT:
            self.copy_x(d, e).wait_recv()
            total = total + self.in2[direct_slot(d, e)].astype(F32)
        return total

    def got_y(self, side, hop):
        self.copy_y(side, hop).wait_recv()
        return self.in1[side * LONG + hop - 1].astype(F32)

    def step(self, depth):
        for side in (0, 1):
            if depth <= HOPS[side]:
                total = self.column_sum(depth if side == 0 else -depth)
                if depth < HOPS[side]:
                    total = total + self.got_y(side, depth + 1)
                self.out1[side * LONG + depth - 1] = total.astype(BF16)
                self.copy_y(side, depth).start()

    def result(self):
        return self.column_sum(0) + self.got_y(0, 1) + self.got_y(1, 1)

    def drain(self):
        for side in (0, 1):
            for hop in range(1, HOPS[side] + 1):
                self.copy_y(side, hop).wait_send()
        for d in FAR_FIRST:
            for e in DIRECT:
                self.copy_x(d, e).wait_send()


class ScatterXY:
    def __init__(self, t, part, out1, in1, out2, in2, s1, r1, s2, r2):
        self.t, self.part, self.out1, self.in1, self.out2, self.in2 = t, part, out1, in1, out2, in2
        self.s1, self.r1, self.s2, self.r2 = s1, r1, s2, r2

    def copy_y(self, d, side, hop):
        sgn = sign(d, side)
        slot = chain_slot(d, side, hop)
        if hop == HOPS[side]:
            src = self.part.at[self.t.yx(-sgn * hop, -d)]
        else:
            src = self.out2.at[slot]
        return remote(src, self.in2.at[slot], self.s2.at[slot], self.r2.at[slot], self.t.device(-sgn, 0))

    def copy_x(self, e):
        slot = DIRECT.index(e)
        return remote(self.out1.at[slot], self.in1.at[slot], self.s1.at[slot], self.r1.at[slot], self.t.device(0, -e))

    def open(self, off):
        for d in (2, 1, -1, 0):
            for side in (0, 1):
                if HOPS[side] == abs(off) and (sign(d, side) * HOPS[side] - off) % NY == 0:
                    self.copy_y(d, side, HOPS[side]).start()

    def got_y(self, d, side, hop):
        self.copy_y(d, side, hop).wait_recv()
        return self.in2[chain_slot(d, side, hop)].astype(F32)

    def column_sum(self, d):
        return self.part[self.t.yx(0, -d)].astype(F32) + self.got_y(d, 0, 1) + self.got_y(d, 1, 1)

    def step(self, depth):
        for d in (2, 1, -1, 0):
            for side in (0, 1):
                hop = depth - 1
                if 1 <= hop < HOPS[side]:
                    total = self.part[self.t.yx(-sign(d, side) * hop, -d)].astype(F32) + self.got_y(d, side, hop + 1)
                    self.out2[chain_slot(d, side, hop)] = total.astype(BF16)
                    self.copy_y(d, side, hop).start()
            if depth == 1 and d != 0:
                self.out1[DIRECT.index(d)] = self.column_sum(d).astype(BF16)
                self.copy_x(d).start()

    def result(self):
        total = self.column_sum(0)
        for e in DIRECT:
            self.copy_x(e).wait_recv()
            total = total + self.in1[DIRECT.index(e)].astype(F32)
        return total

    def drain(self):
        for e in DIRECT:
            self.copy_x(e).wait_send()
        for d in COLUMNS:
            for side in (0, 1):
                for hop in range(1, HOPS[side] + 1):
                    self.copy_y(d, side, hop).wait_send()


def nt_dot(left, right):
    return lax.dot_general(left, right, (((1,), (1,)), ((), ())), preferred_element_type=F32)


def kernel(grad_ref, gate_ref, up_ref, down_hbm, gw_hbm, uw_hbm, in_grad_ref, down_grad_ref,
           rows, hid, part, gu, down_ref, wcat, rs_out1, rs_in1, rs_out2, rs_in2, hg,
           pair_out, pair_in, z_out, z_in, own,
           h_s1, h_r1, h_s2, h_r2, g_s1, g_r1, g_s2, g_r2, p_s1, p_r1, p_s2, p_r2,
           za_s, za_r, zc_s, zc_r, pair_s, pair_r, zs_s, zs_r, load_sem):
    row, col = lax.axis_index("row"), lax.axis_index("col")
    z, core = row // 2, lax.rem(row, 2)
    y, x = col // NX, lax.rem(col, NX)
    other = 1 - core
    way = 1 - 2 * core
    z_at = lambda off: wrap(z + off, NZ)
    y_at = lambda off: wrap(y + off, NY)
    sibling = (z * 2 + other, col)
    torus = Torus(row, y, x)

    def per_core(fn):
        for which in (0, 1):
            pl.when(core == which)(functools.partial(fn, which))

    partners = [sibling]
    partners += [(z_at(off) * 2 + core, col) for off in range(1, NZ)]
    partners += [torus.device(1, 0), torus.device(-1, 0)] + [torus.device(0, e) for e in DIRECT]
    barrier = pltpu.get_barrier_semaphore()
    for partner in partners:
        pl.semaphore_signal(barrier, inc=1, device_id=partner, device_id_type=MESH)

    loads = [pltpu.make_async_copy(down_hbm, down_ref, load_sem.at[0])]
    for i, (src, size, at) in enumerate(((gw_hbm, HEAD, 0), (uw_hbm, HEAD, HEAD))):
        loads.append(pltpu.make_async_copy(src.at[pl.ds(0, size)], wcat.at[pl.ds(at, size)], load_sem.at[1 + 2 * i]))
        loads.append(pltpu.make_async_copy(
            src.at[pl.ds(HEAD, UNITS - HEAD)], wcat.at[pl.ds(2 * HEAD + i * (UNITS - HEAD), UNITS - HEAD)],
            load_sem.at[2 + 2 * i]))
    for load in loads:
        load.start()

    gate = gate_ref[...].astype(F32)
    sig = jax.nn.sigmoid(gate)
    hid[y, x] = (gate * sig * up_ref[...].astype(F32)).astype(BF16)
    rows[row] = grad_ref[...]
    pl.semaphore_wait(barrier, len(partners))

    def z_copy(off, via=0, to=0):
        ref = rows.at[z_at(-way * (off if to else via)) * 2 + core]
        slot = off + 3
        return remote(ref, ref, za_s.at[slot], za_r.at[slot], (z_at(way * (off - via)) * 2 + core, col))

    def cross_copy(off, which):
        ref = rows.at[z_at(off) * 2 + which]
        return remote(ref, ref, zc_s.at[off + 3], zc_r.at[off + 3], sibling)

    def cross_slot(off, sgn):
        return 4 if abs(off) == 4 else off * sgn

    def hidden_gather(which):
        return (GatherYX, GatherXY)[which](torus, hid, h_s1, h_r1, h_s2, h_r2)

    def grads_gather(which):
        return (GatherYX, GatherXY)[which](torus, gu, g_s1, g_r1, g_s2, g_r2)

    def scatter(which):
        return (ScatterYX, ScatterXY)[which](torus, part, rs_out1, rs_in1, rs_out2, rs_in2, p_s1, p_r1, p_s2, p_r2)

    def z_got(off):
        z_copy(off, 0, 1).wait_recv()

    def z_pass(off):
        def send(which):
            cross_copy(cross_slot(-off, 1 - 2 * which), which).start()

        per_core(send)

    for off in (2, -2, 1, -1):
        z_copy(off).start()
    per_core(lambda which: hidden_gather(which).begin())
    cross_copy(0, core).start()
    z_got(2)
    z_copy(4, 2).start()
    z_copy(3, 2).start()
    z_got(-2)
    z_copy(-3, -2).start()
    for off in (2, -2):
        z_pass(off)
    for off in (1, -1):
        z_got(off)
        z_pass(off)
    for time in (1, 2):
        per_core(lambda which: hidden_gather(which).step(time))
    for off in (3, -3, 4):
        z_got(off)
        z_pass(off)
    for load in loads:
        load.wait()
    for off in range(-3, 5):
        cross_copy(off, other).wait_recv()

    def matmul1(off):
        iz = y_at(off)
        block = rows[pl.ds(iz * 2, 2)].reshape(2 * PAIR, FEAT)
        part[iz] = nt_dot(block, down_ref[...]).astype(BF16).reshape(NX, TOK, UNITS)

    for off in FAR_FIRST:
        matmul1(-off)
        per_core(lambda which: scatter(which).open(off))
    for depth in (4, 3, 2, 1):
        per_core(lambda which: scatter(which).step(depth))
        if depth in AFTER:
            per_core(lambda which: hidden_gather(which).step(AFTER[depth]))

    def finish(which):
        hg[...] = scatter(which).result()

    per_core(finish)
    grad = hg[...]
    upv = up_ref[...].astype(F32)
    ug = (grad * (gate * sig)).astype(BF16)
    gg = (grad * upv * sig * (1.0 + gate * (1.0 - sig))).astype(BF16)
    gu[y, x, :, :HEAD] = gg[:, :HEAD]
    gu[y, x, :, HEAD:2 * HEAD] = ug[:, :HEAD]
    gu[y, x, :, 2 * HEAD:] = jnp.concatenate([gg[:, HEAD:], ug[:, HEAD:]], axis=1)

    per_core(lambda which: grads_gather(which).begin())

    def pair_copy(off):
        slot = off + 3
        return remote(pair_out.at[slot], pair_in.at[slot], pair_s.at[slot], pair_r.at[slot], sibling)

    def z_send(off):
        return remote(z_out.at[off + 3], z_in.at[z], zs_s.at[off + 3], zs_r.at[z], (y_at(off) * 2 + core, col))

    def block(off):
        per_core(lambda which: grads_gather(which).leaves(off))
        both = gu[y_at(off)].reshape(NX * TOK, WIDE)
        total = jnp.dot(both, wcat[...], preferred_element_type=F32)
        lower, upper = total[:PAIR], total[PAIR:]
        own[off + 3] = jnp.where(core == 0, lower, upper)
        pair_out[off + 3] = jnp.where(core == 0, upper, lower).astype(BF16)
        pair_copy(off).start()

    def pass_on(off):
        pair_copy(off).wait_recv()
        total = own[off + 3] + pair_in[off + 3].astype(F32)

        @pl.when(y_at(off) != z)
        def _():
            z_out[off + 3] = total.astype(BF16)
            z_send(off).start()

        @pl.when(y_at(off) == z)
        def _():
            own[8] = total

    for time in (1, 2, 3, 4):
        per_core(lambda which: grads_gather(which).step(time))
        if time == 2:
            block(0)
        if time == 3:
            pass_on(0)
            block(1)
            block(-1)
    pass_on(1)
    pass_on(-1)
    def hidden_leaves(which):
        for off in FAR_FIRST:
            hidden_gather(which).leaves(off)

    per_core(hidden_leaves)
    all_rows = rows[...].reshape(NZ * 2 * PAIR, FEAT)
    for start, size in ((0, 256), (256, 256), (512, 320)):
        units = hid[:, :, :, pl.ds(start, size)].reshape(NY * NX * TOK, size)
        down_grad_ref[pl.ds(start, size)] = lax.dot_general(
            units, all_rows, (((0,), (0,)), ((), ())), preferred_element_type=F32).astype(BF16)

    for off in (2, -2):
        block(off)
    for off in (2, -2):
        pass_on(off)
    for off in (3, -3):
        block(off)
    for off in (3, -3):
        pass_on(off)
    block(4)
    pass_on(4)

    total = own[8]
    for off in range(1, NZ):
        iz = z_at(off)
        ref = z_in.at[iz]
        remote(ref, ref, zs_s.at[0], zs_r.at[iz], (iz * 2 + core, col)).wait_recv()
        total = total + ref[...].astype(F32)
    in_grad_ref[...] = total.astype(BF16)

    for off, via in ((2, 0), (-2, 0), (1, 0), (-1, 0), (4, 2), (3, 2), (-3, -2)):
        z_copy(off, via).wait_send()
    for off in range(-3, 5):
        cross_copy(off, core).wait_send()
        pair_copy(off).wait_send()
        pl.when(y_at(off) != z)(lambda: z_send(off).wait_send())

    def drain(which):
        hidden_gather(which).drain()
        scatter(which).drain()
        grads_gather(which).drain()

    per_core(drain)


def copy_out(a_ref, b_ref, a_out, b_out):
    a_out[...] = a_ref[...]
    b_out[...] = b_ref[...]


def on_device(grad_out, gate_pre, up_pre, down_weight, gate_weight, up_weight):
    vmem, anywhere = pl.BlockSpec(memory_space=pltpu.VMEM), pl.BlockSpec(memory_space=pl.ANY)
    dma = pltpu.SemaphoreType.DMA
    tree_sems = [dma((8,)), dma((8,)), dma((32,)), dma((32,))]
    outs = (jax.ShapeDtypeStruct((PAIR, FEAT), BF16), jax.ShapeDtypeStruct((UNITS, FEAT), BF16))
    input_grad, down_grad = pl.pallas_call(
        kernel,
        out_shape=outs,
        in_specs=[vmem] * 3 + [anywhere] * 3,
        out_specs=(vmem, vmem),
        scratch_shapes=[
            pltpu.VMEM((2 * NZ, PAIR, FEAT), BF16),
            pltpu.VMEM((NY, NX, TOK, UNITS), BF16),
            pltpu.VMEM((NY, NX, TOK, UNITS), BF16),
            pltpu.VMEM((NY, NX, TOK, WIDE), BF16),
            pltpu.VMEM((UNITS, FEAT), BF16),
            pltpu.VMEM((WIDE, FEAT), BF16),
            pltpu.VMEM((8, TOK, UNITS), BF16),
            pltpu.VMEM((8, TOK, UNITS), BF16),
            pltpu.VMEM((32, TOK, UNITS), BF16),
            pltpu.VMEM((32, TOK, UNITS), BF16),
            pltpu.VMEM((TOK, UNITS), F32),
            pltpu.VMEM((8, PAIR, FEAT), BF16),
            pltpu.VMEM((8, PAIR, FEAT), BF16),
            pltpu.VMEM((8, PAIR, FEAT), BF16),
            pltpu.VMEM((8, PAIR, FEAT), BF16),
            pltpu.VMEM((9, PAIR, FEAT), F32),
        ] + tree_sems * 3 + [dma((8,))] * 8 + [dma((5,))],
        compiler_params=pltpu.CompilerParams(
            collective_id=0, has_side_effects=True, vmem_limit_bytes=56 * 2**20),
        cost_estimate=pl.CostEstimate(flops=5_234_491_392, bytes_accessed=4_000_000, transcendentals=40_000),
    )(grad_out, gate_pre, up_pre, down_weight, gate_weight.T, up_weight.T)
    return pl.pallas_call(
        copy_out,
        out_shape=outs,
        in_specs=[vmem] * 2,
        out_specs=(vmem, vmem),
    )(input_grad, down_grad)


def solution(mesh):
    placed = (
        P("row", "col"),
        P("col", "row"),
        P("col", "row"),
        P("row", "col"),
        P("col", "row"),
        P("col", "row"),
    )
    return jax.shard_map(
        on_device,
        mesh=mesh,
        in_specs=placed,
        out_specs=(P("row", "col"), P("row", "col")),
        check_vma=False,
    )
```

```python
import functools

import jax
import jax.numpy as jnp
from jax import lax
from jax.experimental import pallas as pl
from jax.experimental.pallas import tpu as pltpu
from jax.sharding import PartitionSpec as P

NZ, NY, NX = 8, 8, 4
TOK = 48
PAIR = 96
UNITS = 832
WIDE = 2 * UNITS
HEAD = 768
FEAT = 512
MESH = pl.DeviceIdType.MESH
F32, BF16 = jnp.float32, jnp.bfloat16


def wrap(value, size):
    return lax.rem(value + 2 * size, size)


class Torus:
    def __init__(self, row, y, x):
        self.row, self.y, self.x = row, y, x

    def yx(self, off_y, off_x):
        return wrap(self.y + off_y, NY), wrap(self.x + off_x, NX)

    def device(self, off_y, off_x):
        iy, ix = self.yx(off_y, off_x)
        return (self.row, iy * NX + ix)


LONG = NY // 2
HOPS = (LONG, LONG - 1)
DIRECT = (2, 1, -1)
AFTER = {4: 3, 1: 4}
COLUMNS = (0, 1, -1, 2)


def y_offsets(dist):
    return [dist] if dist in (0, LONG) else [dist, -dist]


FAR_FIRST = [d for dist in range(LONG, -1, -1) for d in y_offsets(dist)]


def sign(d, side):
    return 1 - 2 * ((d + side) % 2)


def chain_slot(d, side, hop):
    return (side * LONG + hop - 1) * 4 + d + 1


def direct_slot(d, e):
    return DIRECT.index(e) * 8 + d + 3


def remote(src, dst, send, recv, device):
    return pltpu.make_async_remote_copy(
        src_ref=src, dst_ref=dst, send_sem=send, recv_sem=recv, device_id=device, device_id_type=MESH)


class GatherYX:
    def __init__(self, t, buf, s1, r1, s2, r2):
        self.t, self.buf, self.s1, self.r1, self.s2, self.r2 = t, buf, s1, r1, s2, r2

    def ref(self, off_y, off_x):
        return self.buf.at[self.t.yx(off_y, off_x)]

    def copy_y(self, side, hop, to=0):
        sgn = 1 - 2 * side
        ref = self.ref(-sgn * (hop - 1 + to), 0)
        slot = side * LONG + hop - 1
        return remote(ref, ref, self.s1.at[slot], self.r1.at[slot], self.t.device(sgn, 0))

    def copy_x(self, d, e, to=0):
        ref = self.ref(-d, -e * to)
        slot = direct_slot(d, e)
        return remote(ref, ref, self.s2.at[slot], self.r2.at[slot], self.t.device(0, e))

    def open(self, d):
        for e in DIRECT:
            self.copy_x(d, e).start()

    def begin(self):
        for side in (0, 1):
            self.copy_y(side, 1).start()
        self.open(0)

    def step(self, time):
        for side in (0, 1):
            if time <= HOPS[side]:
                self.copy_y(side, time, 1).wait_recv()
                if time < HOPS[side]:
                    self.copy_y(side, time + 1).start()
        for side in (0, 1):
            if time <= HOPS[side]:
                self.open(time if side == 0 else -time)

    def leaves(self, off):
        for e in DIRECT:
            self.copy_x(off if off == LONG else -off, e, 1).wait_recv()

    def drain(self):
        for side in (0, 1):
            for hop in range(1, HOPS[side] + 1):
                self.copy_y(side, hop).wait_send()
        for d in FAR_FIRST:
            for e in DIRECT:
                self.copy_x(d, e).wait_send()


class GatherXY:
    def __init__(self, t, buf, s1, r1, s2, r2):
        self.t, self.buf, self.s1, self.r1, self.s2, self.r2 = t, buf, s1, r1, s2, r2

    def ref(self, off_y, off_x):
        return self.buf.at[self.t.yx(off_y, off_x)]

    def copy_x(self, e, to=0):
        ref = self.ref(0, -e * to)
        slot = DIRECT.index(e)
        return remote(ref, ref, self.s1.at[slot], self.r1.at[slot], self.t.device(0, e))

    def copy_y(self, d, side, hop, to=0):
        sgn = sign(d, side)
        ref = self.ref(-sgn * (hop - 1 + to), -d)
        slot = chain_slot(d, side, hop)
        return remote(ref, ref, self.s2.at[slot], self.r2.at[slot], self.t.device(sgn, 0))

    def begin(self):
        for e in DIRECT:
            self.copy_x(e).start()
        for side in (0, 1):
            self.copy_y(0, side, 1).start()

    def step(self, time):
        if time == 1:
            for e in (1, -1, 2):
                self.copy_x(e, 1).wait_recv()
                for side in (0, 1):
                    self.copy_y(e, side, 1).start()
        for d in COLUMNS:
            hop = time if d == 0 else time - 1
            for side in (0, 1):
                if 1 <= hop < HOPS[side]:
                    self.copy_y(d, side, hop, 1).wait_recv()
                    self.copy_y(d, side, hop + 1).start()

    def leaves(self, off):
        for d in COLUMNS:
            for side in (0, 1):
                hop = HOPS[side]
                if hop == abs(off) and (-sign(d, side) * hop - off) % NY == 0:
                    self.copy_y(d, side, hop, 1).wait_recv()

    def drain(self):
        for e in DIRECT:
            self.copy_x(e).wait_send()
        for d in COLUMNS:
            for side in (0, 1):
                for hop in range(1, HOPS[side] + 1):
                    self.copy_y(d, side, hop).wait_send()


class ScatterYX:
    def __init__(self, t, part, out1, in1, out2, in2, s1, r1, s2, r2):
        self.t, self.part, self.out1, self.in1, self.in2 = t, part, out1, in1, in2
        self.s1, self.r1, self.s2, self.r2 = s1, r1, s2, r2

    def copy_x(self, d, e):
        slot = direct_slot(d, e)
        return remote(self.part.at[self.t.yx(-d, -e)], self.in2.at[slot], self.s2.at[slot], self.r2.at[slot],
                      self.t.device(0, -e))

    def copy_y(self, side, hop):
        slot = side * LONG + hop - 1
        return remote(self.out1.at[slot], self.in1.at[slot], self.s1.at[slot], self.r1.at[slot],
                      self.t.device(-1 + 2 * side, 0))

    def open(self, d):
        for e in DIRECT:
            self.copy_x(d, e).start()

    def column_sum(self, d):
        total = self.part[self.t.yx(-d, 0)].astype(F32)
        for e in DIRECT:
            self.copy_x(d, e).wait_recv()
            total = total + self.in2[direct_slot(d, e)].astype(F32)
        return total

    def got_y(self, side, hop):
        self.copy_y(side, hop).wait_recv()
        return self.in1[side * LONG + hop - 1].astype(F32)

    def step(self, depth):
        for side in (0, 1):
            if depth <= HOPS[side]:
                total = self.column_sum(depth if side == 0 else -depth)
                if depth < HOPS[side]:
                    total = total + self.got_y(side, depth + 1)
                self.out1[side * LONG + depth - 1] = total.astype(BF16)
                self.copy_y(side, depth).start()

    def result(self):
        return self.column_sum(0) + self.got_y(0, 1) + self.got_y(1, 1)

    def drain(self):
        for side in (0, 1):
            for hop in range(1, HOPS[side] + 1):
                self.copy_y(side, hop).wait_send()
        for d in FAR_FIRST:
            for e in DIRECT:
                self.copy_x(d, e).wait_send()


class ScatterXY:
    def __init__(self, t, part, out1, in1, out2, in2, s1, r1, s2, r2):
        self.t, self.part, self.out1, self.in1, self.out2, self.in2 = t, part, out1, in1, out2, in2
        self.s1, self.r1, self.s2, self.r2 = s1, r1, s2, r2

    def copy_y(self, d, side, hop):
        sgn = sign(d, side)
        slot = chain_slot(d, side, hop)
        if hop == HOPS[side]:
            src = self.part.at[self.t.yx(-sgn * hop, -d)]
        else:
            src = self.out2.at[slot]
        return remote(src, self.in2.at[slot], self.s2.at[slot], self.r2.at[slot], self.t.device(-sgn, 0))

    def copy_x(self, e):
        slot = DIRECT.index(e)
        return remote(self.out1.at[slot], self.in1.at[slot], self.s1.at[slot], self.r1.at[slot], self.t.device(0, -e))

    def open(self, off):
        for d in (2, 1, -1, 0):
            for side in (0, 1):
                if HOPS[side] == abs(off) and (sign(d, side) * HOPS[side] - off) % NY == 0:
                    self.copy_y(d, side, HOPS[side]).start()

    def got_y(self, d, side, hop):
        self.copy_y(d, side, hop).wait_recv()
        return self.in2[chain_slot(d, side, hop)].astype(F32)

    def column_sum(self, d):
        return self.part[self.t.yx(0, -d)].astype(F32) + self.got_y(d, 0, 1) + self.got_y(d, 1, 1)

    def step(self, depth):
        for d in (2, 1, -1, 0):
            for side in (0, 1):
                hop = depth - 1
                if 1 <= hop < HOPS[side]:
                    total = self.part[self.t.yx(-sign(d, side) * hop, -d)].astype(F32) + self.got_y(d, side, hop + 1)
                    self.out2[chain_slot(d, side, hop)] = total.astype(BF16)
                    self.copy_y(d, side, hop).start()
            if depth == 1 and d != 0:
                self.out1[DIRECT.index(d)] = self.column_sum(d).astype(BF16)
                self.copy_x(d).start()

    def result(self):
        total = self.column_sum(0)
        for e in DIRECT:
            self.copy_x(e).wait_recv()
            total = total + self.in1[DIRECT.index(e)].astype(F32)
        return total

    def drain(self):
        for e in DIRECT:
            self.copy_x(e).wait_send()
        for d in COLUMNS:
            for side in (0, 1):
                for hop in range(1, HOPS[side] + 1):
                    self.copy_y(d, side, hop).wait_send()


def nt_dot(left, right):
    return lax.dot_general(left, right, (((1,), (1,)), ((), ())), preferred_element_type=F32)


def kernel(grad_ref, gate_ref, up_ref, down_hbm, gw_hbm, uw_hbm, in_grad_ref, down_grad_ref,
           rows, hid, part, gu, down_ref, wcat, rs_out1, rs_in1, rs_out2, rs_in2, hg,
           pair_out, pair_in, z_out, z_in, own,
           h_s1, h_r1, h_s2, h_r2, g_s1, g_r1, g_s2, g_r2, p_s1, p_r1, p_s2, p_r2,
           za_s, za_r, zc_s, zc_r, pair_s, pair_r, zs_s, zs_r, load_sem):
    row, col = lax.axis_index("row"), lax.axis_index("col")
    z, core = row // 2, lax.rem(row, 2)
    y, x = col // NX, lax.rem(col, NX)
    other = 1 - core
    way = 1 - 2 * core
    z_at = lambda off: wrap(z + off, NZ)
    y_at = lambda off: wrap(y + off, NY)
    sibling = (z * 2 + other, col)
    torus = Torus(row, y, x)

    def per_core(fn):
        for which in (0, 1):
            pl.when(core == which)(functools.partial(fn, which))

    partners = [sibling]
    partners += [(z_at(off) * 2 + core, col) for off in range(1, NZ)]
    partners += [torus.device(1, 0), torus.device(-1, 0)] + [torus.device(0, e) for e in DIRECT]
    barrier = pltpu.get_barrier_semaphore()
    for partner in partners:
        pl.semaphore_signal(barrier, inc=1, device_id=partner, device_id_type=MESH)

    loads = [pltpu.make_async_copy(down_hbm, down_ref, load_sem.at[0])]
    for i, (src, size, at) in enumerate(((gw_hbm, HEAD, 0), (uw_hbm, HEAD, HEAD))):
        loads.append(pltpu.make_async_copy(src.at[pl.ds(0, size)], wcat.at[pl.ds(at, size)], load_sem.at[1 + 2 * i]))
        loads.append(pltpu.make_async_copy(
            src.at[pl.ds(HEAD, UNITS - HEAD)], wcat.at[pl.ds(2 * HEAD + i * (UNITS - HEAD), UNITS - HEAD)],
            load_sem.at[2 + 2 * i]))
    for load in loads:
        load.start()

    gate = gate_ref[...].astype(F32)
    sig = jax.nn.sigmoid(gate)
    hid[y, x] = (gate * sig * up_ref[...].astype(F32)).astype(BF16)
    rows[row] = grad_ref[...]
    pl.semaphore_wait(barrier, len(partners))

    def z_copy(off, via=0, to=0):
        ref = rows.at[z_at(-way * (off if to else via)) * 2 + core]
        slot = off + 3
        return remote(ref, ref, za_s.at[slot], za_r.at[slot], (z_at(way * (off - via)) * 2 + core, col))

    def cross_copy(off, which):
        ref = rows.at[z_at(off) * 2 + which]
        return remote(ref, ref, zc_s.at[off + 3], zc_r.at[off + 3], sibling)

    def cross_slot(off, sgn):
        return 4 if abs(off) == 4 else off * sgn

    def hidden_gather(which):
        return (GatherYX, GatherXY)[which](torus, hid, h_s1, h_r1, h_s2, h_r2)

    def grads_gather(which):
        return (GatherYX, GatherXY)[which](torus, gu, g_s1, g_r1, g_s2, g_r2)

    def scatter(which):
        return (ScatterYX, ScatterXY)[which](torus, part, rs_out1, rs_in1, rs_out2, rs_in2, p_s1, p_r1, p_s2, p_r2)

    def z_got(off):
        z_copy(off, 0, 1).wait_recv()

    def z_pass(off):
        def send(which):
            cross_copy(cross_slot(-off, 1 - 2 * which), which).start()

        per_core(send)

    for off in (2, -2, 1, -1):
        z_copy(off).start()
    per_core(lambda which: hidden_gather(which).begin())
    cross_copy(0, core).start()
    z_got(2)
    z_copy(4, 2).start()
    z_copy(3, 2).start()
    z_got(-2)
    z_copy(-3, -2).start()
    for off in (2, -2):
        z_pass(off)
    for off in (1, -1):
        z_got(off)
        z_pass(off)
    for time in (1, 2):
        per_core(lambda which: hidden_gather(which).step(time))
    for off in (3, -3, 4):
        z_got(off)
        z_pass(off)
    for load in loads:
        load.wait()
    for off in range(-3, 5):
        cross_copy(off, other).wait_recv()

    def matmul1(off):
        iz = y_at(off)
        block = rows[pl.ds(iz * 2, 2)].reshape(2 * PAIR, FEAT)
        part[iz] = nt_dot(block, down_ref[...]).astype(BF16).reshape(NX, TOK, UNITS)

    for off in FAR_FIRST:
        matmul1(-off)
        per_core(lambda which: scatter(which).open(off))
    for depth in (4, 3, 2, 1):
        per_core(lambda which: scatter(which).step(depth))
        if depth in AFTER:
            per_core(lambda which: hidden_gather(which).step(AFTER[depth]))

    def finish(which):
        hg[...] = scatter(which).result()

    per_core(finish)
    grad = hg[...]
    upv = up_ref[...].astype(F32)
    ug = (grad * (gate * sig)).astype(BF16)
    gg = (grad * upv * sig * (1.0 + gate * (1.0 - sig))).astype(BF16)
    gu[y, x, :, :HEAD] = gg[:, :HEAD]
    gu[y, x, :, HEAD:2 * HEAD] = ug[:, :HEAD]
    gu[y, x, :, 2 * HEAD:] = jnp.concatenate([gg[:, HEAD:], ug[:, HEAD:]], axis=1)

    per_core(lambda which: grads_gather(which).begin())

    def pair_copy(off):
        slot = off + 3
        return remote(pair_out.at[slot], pair_in.at[slot], pair_s.at[slot], pair_r.at[slot], sibling)

    def z_send(off):
        return remote(z_out.at[off + 3], z_in.at[z], zs_s.at[off + 3], zs_r.at[z], (y_at(off) * 2 + core, col))

    def block(off):
        per_core(lambda which: grads_gather(which).leaves(off))
        both = gu[y_at(off)].reshape(NX * TOK, WIDE)
        total = jnp.dot(both, wcat[...], preferred_element_type=F32)
        lower, upper = total[:PAIR], total[PAIR:]
        own[off + 3] = jnp.where(core == 0, lower, upper)
        pair_out[off + 3] = jnp.where(core == 0, upper, lower).astype(BF16)
        pair_copy(off).start()

    def pass_on(off):
        pair_copy(off).wait_recv()
        total = own[off + 3] + pair_in[off + 3].astype(F32)

        @pl.when(y_at(off) != z)
        def _():
            z_out[off + 3] = total.astype(BF16)
            z_send(off).start()

        @pl.when(y_at(off) == z)
        def _():
            own[8] = total

    for time in (1, 2, 3, 4):
        per_core(lambda which: grads_gather(which).step(time))
        if time >= 2:
            for off in y_offsets(time - 2):
                pass_on(off)
        if time <= 3:
            for off in y_offsets(time - 1):
                block(off)
    def hidden_leaves(which):
        for off in FAR_FIRST:
            hidden_gather(which).leaves(off)

    per_core(hidden_leaves)
    all_rows = rows[...].reshape(NZ * 2 * PAIR, FEAT)
    for start, size in ((0, 256), (256, 256), (512, 320)):
        units = hid[:, :, :, pl.ds(start, size)].reshape(NY * NX * TOK, size)
        down_grad_ref[pl.ds(start, size)] = lax.dot_general(
            units, all_rows, (((0,), (0,)), ((), ())), preferred_element_type=F32).astype(BF16)

    for off in (3, -3):
        block(off)
    for off in (3, -3):
        pass_on(off)
    block(4)
    pass_on(4)

    total = own[8]
    for off in range(1, NZ):
        iz = z_at(off)
        ref = z_in.at[iz]
        remote(ref, ref, zs_s.at[0], zs_r.at[iz], (iz * 2 + core, col)).wait_recv()
        total = total + ref[...].astype(F32)
    in_grad_ref[...] = total.astype(BF16)

    for off, via in ((2, 0), (-2, 0), (1, 0), (-1, 0), (4, 2), (3, 2), (-3, -2)):
        z_copy(off, via).wait_send()
    for off in range(-3, 5):
        cross_copy(off, core).wait_send()
        pair_copy(off).wait_send()
        pl.when(y_at(off) != z)(lambda: z_send(off).wait_send())

    def drain(which):
        hidden_gather(which).drain()
        scatter(which).drain()
        grads_gather(which).drain()

    per_core(drain)


def copy_out(a_ref, b_ref, a_out, b_out):
    a_out[...] = a_ref[...]
    b_out[...] = b_ref[...]


def on_device(grad_out, gate_pre, up_pre, down_weight, gate_weight, up_weight):
    vmem, anywhere = pl.BlockSpec(memory_space=pltpu.VMEM), pl.BlockSpec(memory_space=pl.ANY)
    dma = pltpu.SemaphoreType.DMA
    tree_sems = [dma((8,)), dma((8,)), dma((32,)), dma((32,))]
    outs = (jax.ShapeDtypeStruct((PAIR, FEAT), BF16), jax.ShapeDtypeStruct((UNITS, FEAT), BF16))
    input_grad, down_grad = pl.pallas_call(
        kernel,
        out_shape=outs,
        in_specs=[vmem] * 3 + [anywhere] * 3,
        out_specs=(vmem, vmem),
        scratch_shapes=[
            pltpu.VMEM((2 * NZ, PAIR, FEAT), BF16),
            pltpu.VMEM((NY, NX, TOK, UNITS), BF16),
            pltpu.VMEM((NY, NX, TOK, UNITS), BF16),
            pltpu.VMEM((NY, NX, TOK, WIDE), BF16),
            pltpu.VMEM((UNITS, FEAT), BF16),
            pltpu.VMEM((WIDE, FEAT), BF16),
            pltpu.VMEM((8, TOK, UNITS), BF16),
            pltpu.VMEM((8, TOK, UNITS), BF16),
            pltpu.VMEM((32, TOK, UNITS), BF16),
            pltpu.VMEM((32, TOK, UNITS), BF16),
            pltpu.VMEM((TOK, UNITS), F32),
            pltpu.VMEM((8, PAIR, FEAT), BF16),
            pltpu.VMEM((8, PAIR, FEAT), BF16),
            pltpu.VMEM((8, PAIR, FEAT), BF16),
            pltpu.VMEM((8, PAIR, FEAT), BF16),
            pltpu.VMEM((9, PAIR, FEAT), F32),
        ] + tree_sems * 3 + [dma((8,))] * 8 + [dma((5,))],
        compiler_params=pltpu.CompilerParams(
            collective_id=0, has_side_effects=True, vmem_limit_bytes=56 * 2**20),
        cost_estimate=pl.CostEstimate(flops=5_234_491_392, bytes_accessed=4_000_000, transcendentals=40_000),
    )(grad_out, gate_pre, up_pre, down_weight, gate_weight.T, up_weight.T)
    return pl.pallas_call(
        copy_out,
        out_shape=outs,
        in_specs=[vmem] * 2,
        out_specs=(vmem, vmem),
    )(input_grad, down_grad)


def solution(mesh):
    placed = (
        P("row", "col"),
        P("col", "row"),
        P("col", "row"),
        P("row", "col"),
        P("col", "row"),
        P("col", "row"),
    )
    return jax.shard_map(
        on_device,
        mesh=mesh,
        in_specs=placed,
        out_specs=(P("row", "col"), P("row", "col")),
        check_vma=False,
    )
```
